32 devices in a mesh: wide: 8 (over z, y), narrow: 4 (over x, core).
Axes of the slice: x: 2, y: 2, z: 4, core: 2. Of those that a mesh axis runs over, the one named last changes fastest.
Arguments:
- labels: int32 [256, 128, 128], P('narrow', 'wide'), may hold values 0 or 1
- density: float32 [256, 128, 128], P('narrow', 'wide'), may hold values from 0.9 to 1.1
- velocity: float32 [3, 256, 128, 128], P(None, 'narrow', 'wide'), may hold values from 0.05 to 0.2
- owner_map: int32 [16, 8, 8], P('narrow'), may hold values from 0 to 7, as said below
Outputs:
- moments: float32 [4, 4, 8, 40, 4096], P(None, 'narrow', 'wide')
The draws below stay inside these ranges and needn't reach their ends.
Inputs may be any that keep to these rules, and one draw needn't show every extreme that they name: owner_map[g_x, g_y, g_z] is the wide index of the device that receives block (g_x, g_y, g_z), whose image brick lies on the device with narrow index g_x // 4 and wide index g_y; the receiver has that same narrow index. From one device's brick at most 2 blocks go to any one other receiver, and in every draw some pair has 2; one device receives at most 40 blocks, and in every draw some device receives 40.
All inputs are finite; a program needn't handle non-finite values. No bound on the sum of `labels` on one device may be relied on, other than what follows from the above.
Results may differ from the reference program's by a relative error of at most 0.00002.
Values sent between devices are 32-bit elements; how exact they have to be, the bound alone decides.
A program may use at most 192 MiB of HBM per device.

```python
import math
import jax
import jax.numpy as jnp

BS = 16
RADIUS = 2
STEPS = 4
BXL = 4
BZD = 8
NX = 256
NY = 128
NZ = 128
BLK = 32
CAP = 40
N_WIDE = 8
N_NARROW = 4


def shuffled_order(order_key):
    return jax.random.permutation(order_key, BXL * BZD)


def owner_column(column_key):
    wide_count = N_WIDE
    groups = wide_count - 1
    pair_count = groups // 2
    block_count = BXL * BZD
    key_pair, key_single, key_target, key_order = jax.random.split(column_key, 4)
    first_size = jax.random.randint(key_pair, (wide_count, pair_count), 0, 3)
    group_ids = jnp.arange(groups, dtype=jnp.int32)[None, :]
    is_odd = group_ids % 2
    in_pair = group_ids < 2 * pair_count
    pair_index = jnp.minimum(group_ids // 2, pair_count - 1)
    paired = first_size[:, pair_index[0]]
    paired = jnp.where(is_odd == 1, 2 - paired, paired)
    single = jax.random.randint(key_single, (wide_count, groups), 0, 3)
    group_size = jnp.where(in_pair, paired, single)
    target = jax.random.randint(key_target, (), 0, wide_count)
    sources = jnp.arange(wide_count, dtype=jnp.int32)[:, None]
    forced = (target - sources - 1) % wide_count
    partner = jnp.where(forced < 2 * pair_count, forced ^ 1, -1)
    group_size = jnp.where(group_ids == forced, 2, jnp.where(group_ids == partner, 0, group_size))
    group_size = jnp.where((sources == target) & jnp.logical_not(in_pair), 0, group_size)
    sent_total = jnp.sum(group_size, axis=1)
    group_end = jnp.cumsum(group_size, axis=1)
    order_keys = jax.random.split(key_order, wide_count)
    orders = jax.vmap(shuffled_order)(order_keys)
    places = jnp.arange(block_count, dtype=jnp.int32)[None, :]
    group_of = jnp.sum(group_end[:, None, :] <= places[:, :, None], axis=2).astype(jnp.int32)
    target_of = jnp.where(places < sent_total[:, None], (sources + group_of + 1) % wide_count, sources)
    owners = jnp.zeros((wide_count, block_count), jnp.int32).at[sources, orders].set(target_of.astype(jnp.int32))
    return owners.reshape(wide_count, BXL, BZD).transpose(1, 0, 2)


def draw_owner_map(key, part):
    columns = [owner_column(jax.random.fold_in(key, 101 + column_no)) for column_no in range(N_NARROW)]
    return jnp.concatenate(columns, axis=0).astype(jnp.int32)


def place_ends(values, stream_key, smallest, high):
    index_at = [jax.random.randint(jax.random.fold_in(stream_key, axis), (), 0, length) for axis, length in enumerate(values.shape)]
    main_axis = values.shape.index(max(values.shape))
    neighbour = index_at[:main_axis] + [(index_at[main_axis] + 1) % values.shape[main_axis]] + index_at[main_axis + 1:]
    return values.at[tuple(index_at)].set(smallest).at[tuple(neighbour)].set(high)


def level_of(key, extent, shards, least, top_value):
    level = 1.0
    for axis_at, blocks in shards:
        draws = jax.random.uniform(jax.random.fold_in(jax.random.fold_in(key, 6), axis_at), (blocks,), jnp.float32, least / len(shards), top_value / len(shards))
        level = level * jnp.repeat(jnp.exp(draws), extent[axis_at] // blocks).reshape((-1,) + (1,) * (len(extent) - 1 - axis_at))
    return level


def setup_inputs(seed: int = 0) -> dict:
    seeds = jax.random.split(jax.random.key(seed), 5)
    return {
        "labels": place_ends((jax.random.randint(seeds[0], (NX, NY, NZ), 0, 5) < 2).astype(jnp.int32), jax.random.fold_in(seeds[0], 1), 0, 1),
        "density": jnp.clip(0.9 + 0.20000005 * jax.random.uniform(seeds[1], (NX, NY, NZ), jnp.float32) ** level_of(seeds[1], (NX, NY, NZ), ((0, 4), (1, 8)), -0.2, 0.2), 0.9, 1.1),
        "velocity": jnp.clip(0.05 + 0.15 * jax.random.uniform(seeds[2], (3, NX, NY, NZ), jnp.float32) ** level_of(seeds[2], (3, NX, NY, NZ), ((1, 4), (2, 8)), -0.2, 0.2), 0.05, 0.2),
        "owner_map": draw_owner_map(jax.random.fold_in(seeds[4], 71), 0),
    }


VELOCITIES = ((0, 0, 0), (1, 0, 0), (-1, 0, 0), (0, 1, 0), (0, -1, 0), (0, 0, 1), (0, 0, -1),
              (1, 1, 0), (-1, -1, 0), (1, -1, 0), (-1, 1, 0), (1, 0, 1), (-1, 0, -1),
              (1, 0, -1), (-1, 0, 1), (0, 1, 1), (0, -1, -1), (0, 1, -1), (0, -1, 1))
LATTICE_WEIGHTS = (1.0 / 3.0,) + (1.0 / 18.0,) * 6 + (1.0 / 36.0,) * 12
OPPOSITE = (0, 2, 1, 4, 3, 6, 5, 8, 7, 10, 9, 12, 11, 14, 13, 16, 15, 18, 17)
RELAX = 0.8


def gauss_weights(radius):
    raw_values = [math.exp(-0.5 * offset * offset) for offset in range(-radius, radius + 1)]
    running = 0.0
    for element in raw_values:
        running = running + element
    return [element / running for element in raw_values]


def smooth(scalar_field, axis_no, weights, radius):
    running = jnp.zeros_like(scalar_field)
    for offset in range(-radius, radius + 1):
        running = running + weights[offset + radius] * jnp.roll(scalar_field, -offset, axis=axis_no)
    return running


def projected(direction, vel_x, vel_y, vel_z):
    summands = []
    for axis_no, component in enumerate((vel_x, vel_y, vel_z)):
        if VELOCITIES[direction][axis_no] > 0:
            summands.append(component)
        elif VELOCITIES[direction][axis_no] < 0:
            summands.append(-component)
    if len(summands) == 0:
        return None
    running = summands[0]
    for summand in summands[1:]:
        running = running + summand
    return running


def equilibrium(direction, density_now, vel_x, vel_y, vel_z, square):
    along_lane = projected(direction, vel_x, vel_y, vel_z)
    if along_lane is None:
        return LATTICE_WEIGHTS[direction] * density_now * (1.0 - 1.5 * square)
    return LATTICE_WEIGHTS[direction] * density_now * (
        1.0 + 3.0 * along_lane + 4.5 * along_lane * along_lane - 1.5 * square)


def moment(fields, axis_no):
    running = None
    for direction in range(19):
        facing = VELOCITIES[direction][axis_no]
        if facing == 0:
            continue
        if running is None:
            if facing > 0:
                running = fields[direction]
            else:
                running = -fields[direction]
        else:
            if facing > 0:
                running = running + fields[direction]
            else:
                running = running - fields[direction]
    return running


def relax_cells(fields, greyness, occupied):
    density_now = fields[0]
    for direction in range(1, 19):
        density_now = density_now + fields[direction]
    moment_x = moment(fields, 0)
    moment_y = moment(fields, 1)
    moment_z = moment(fields, 2)
    if occupied is None:
        divisor = density_now
    else:
        divisor = jnp.where(occupied, density_now, 1.0)
    vel_x = moment_x / divisor
    vel_y = moment_y / divisor
    vel_z = moment_z / divisor
    square = vel_x * vel_x + vel_y * vel_y + vel_z * vel_z
    collided = []
    for direction in range(19):
        balance = equilibrium(direction, density_now, vel_x, vel_y, vel_z, square)
        relaxed = fields[direction] - (fields[direction] - balance) / RELAX
        collided.append((1.0 - greyness) * relaxed + greyness * fields[OPPOSITE[direction]])
    return collided


def totals(fields):
    density_now = fields[0]
    for direction in range(1, 19):
        density_now = density_now + fields[direction]
    return jnp.stack([density_now, moment(fields, 0), moment(fields, 1), moment(fields, 2)])


def pack_slots(final, owner_map):
    cube_cells = BS * BS * BS
    blocks = final.reshape(4, N_NARROW, BXL, BS, N_WIDE, BS, BZD, BS)
    blocks = blocks.transpose(1, 4, 2, 6, 0, 3, 5, 7).reshape(N_NARROW, N_WIDE * BLK, 4, cube_cells)
    owners = owner_map.reshape(N_NARROW, BXL, N_WIDE, BZD).transpose(0, 2, 1, 3)
    owners = owners.reshape(N_NARROW, N_WIDE * BLK).astype(jnp.int32)
    numbers = jnp.arange(N_WIDE * BLK, dtype=jnp.int32)
    home_of = (numbers // BLK)[None, :]
    place_of = (numbers % BLK)[None, :]
    stays = owners == home_of
    order_key = jnp.where(stays, place_of, (1 + home_of) * BLK + place_of)
    same_owner = owners[:, :, None] == owners[:, None, :]
    earlier = order_key[:, None, :] < order_key[:, :, None]
    slot_of = jnp.sum(same_owner & earlier, axis=2).astype(jnp.int32)
    column_of = jnp.broadcast_to(jnp.arange(N_NARROW, dtype=jnp.int32)[:, None], owners.shape)
    result = jnp.zeros((4, N_NARROW, N_WIDE, CAP, cube_cells), final.dtype)
    values_in = blocks.reshape(N_NARROW * N_WIDE * BLK, 4, cube_cells).transpose(1, 0, 2)
    return result.at[:, column_of.reshape(-1), owners.reshape(-1), slot_of.reshape(-1), :].set(values_in)


def reference(labels, density, velocity, owner_map):
    weights = gauss_weights(RADIUS)
    greyness = labels.astype(jnp.float32)
    greyness = smooth(greyness, 2, weights, RADIUS)
    greyness = smooth(greyness, 0, weights, RADIUS)
    greyness = smooth(greyness, 1, weights, RADIUS)
    vel_x = velocity[0]
    vel_y = velocity[1]
    vel_z = velocity[2]
    square = vel_x * vel_x + vel_y * vel_y + vel_z * vel_z
    fields = [equilibrium(direction, density, vel_x, vel_y, vel_z, square) for direction in range(19)]
    for step_no in range(STEPS):
        collided = relax_cells(fields, greyness, None)
        fields = [jnp.roll(collided[direction], VELOCITIES[direction], axis=(0, 1, 2))
                  for direction in range(19)]
    return pack_slots(totals(fields), owner_map)
```

```python
import functools
import math

import jax
import jax.numpy as jnp
from jax import lax
from jax.experimental import pallas as pl
from jax.experimental.pallas import tpu as pltpu
from jax.sharding import PartitionSpec as P

BS = 16
RADIUS = 2
STEPS = 4
HALO = STEPS
GHALO = HALO + RADIUS

VELOCITIES = (
    (0, 0, 0),
    (1, 0, 0),
    (-1, 0, 0),
    (0, 1, 0),
    (0, -1, 0),
    (0, 0, 1),
    (0, 0, -1),
    (1, 1, 0),
    (-1, -1, 0),
    (1, -1, 0),
    (-1, 1, 0),
    (1, 0, 1),
    (-1, 0, -1),
    (1, 0, -1),
    (-1, 0, 1),
    (0, 1, 1),
    (0, -1, -1),
    (0, 1, -1),
    (0, -1, 1),
)
MESH = pl.DeviceIdType.MESH


def gauss_weights(radius):
    raw_values = [math.exp(-0.5 * offset * offset) for offset in range(-radius, radius + 1)]
    running = 0.0
    for element in raw_values:
        running = running + element
    return [element / running for element in raw_values]


def dot_c(direction, parts):
    running = None
    for sign, part in zip(VELOCITIES[direction], parts):
        if sign == 0:
            continue
        if running is None:
            running = part if sign > 0 else -part
        else:
            running = running + part if sign > 0 else running - part
    return running


def sums_and_differences(fields):
    sums, diffs = [], []
    mom = [None, None, None]
    rho = fields[0]
    for i in range(1, 19, 2):
        s = fields[i] + fields[i + 1]
        d = fields[i] - fields[i + 1]
        sums.append(s)
        diffs.append(d)
        rho = rho + s
        for axis_no in range(3):
            sign = VELOCITIES[i][axis_no]
            if sign != 0:
                if mom[axis_no] is None:
                    mom[axis_no] = d if sign > 0 else -d
                else:
                    mom[axis_no] = mom[axis_no] + d if sign > 0 else mom[axis_no] - d
    return rho, mom, sums, diffs


def flow_kernel(
    wide_count, narrow_count, X, Y,
    labels, density, velocity, mail_src,
    src_out,
    nat, natl, zs, gx, fld, gext, grey, fa, fb, mom, rows, mail,
    own_sem, xs_sem, xr_sem, ys_sem, yr_sem, as_sem, ar_sem, out_sem,
):
    weights = gauss_weights(RADIUS)
    XE = X + 2 * HALO
    XG = X + 2 * GHALO
    YE = Y + 2 * HALO
    R = XE // 8
    wide = lax.axis_index("wide")
    narrow = lax.axis_index("narrow")
    right = lax.rem(narrow + 1, narrow_count)
    left = lax.rem(narrow + narrow_count - 1, narrow_count)
    up = lax.rem(wide + 1, wide_count)
    down = lax.rem(wide + wide_count - 1, wide_count)

    own = [
        pltpu.make_async_copy(labels, natl.at[pl.ds(GHALO * Y, X * Y)], own_sem.at[0]),
        pltpu.make_async_copy(density, nat.at[pl.ds(0, 1), pl.ds(HALO * Y, X * Y)], own_sem.at[1]),
        pltpu.make_async_copy(velocity, nat.at[pl.ds(1, 3), pl.ds(HALO * Y, X * Y)], own_sem.at[2]),
    ]
    for copy in own:
        copy.start()

    barrier = pltpu.get_barrier_semaphore()
    for target in (left, right):
        pl.semaphore_signal(barrier, inc=1, device_id=(wide, target), device_id_type=MESH)
    for offset in range(1, wide_count):
        pl.semaphore_signal(
            barrier, inc=1, device_id=(lax.rem(wide + offset, wide_count), narrow),
            device_id_type=MESH,
        )
    pl.semaphore_wait(barrier, 2 + wide_count - 1)

    def to_narrow(src, dst, k, target):
        return pltpu.make_async_remote_copy(
            src_ref=src, dst_ref=dst, send_sem=xs_sem.at[k], recv_sem=xr_sem.at[k],
            device_id=(wide, target), device_id_type=MESH,
        )

    xsends = []
    for k, (target, at, to_g, to_f) in enumerate(
        ((right, X, 0, 0), (left, None, X + GHALO, X + HALO))
    ):
        g_at = (X - GHALO) * Y if at is not None else 0
        f_at = (X - HALO) * Y if at is not None else 0
        xsends.append(to_narrow(labels.at[pl.ds(g_at, GHALO * Y)],
                                natl.at[pl.ds(to_g * Y, GHALO * Y)], 3 * k, target))
        xsends.append(to_narrow(density.at[:, pl.ds(f_at, HALO * Y)],
                                nat.at[pl.ds(0, 1), pl.ds(to_f * Y, HALO * Y)], 3 * k + 1, target))
        xsends.append(to_narrow(velocity.at[:, pl.ds(f_at, HALO * Y)],
                                nat.at[pl.ds(1, 3), pl.ds(to_f * Y, HALO * Y)], 3 * k + 2, target))
    for copy in xsends:
        copy.start()

    own[0].wait()
    xsends[0].wait_recv()
    xsends[3].wait_recv()

    def smooth_z(x, carry):
        at = pl.ds(pl.multiple_of(x * Y, 8), Y)
        v = natl[at, :].astype(jnp.float32)
        total = weights[RADIUS] * v
        for k in range(1, RADIUS + 1):
            total = total + weights[RADIUS + k] * (
                pltpu.roll(v, k, 1) + pltpu.roll(v, v.shape[1] - k, 1))
        zs[at, :] = total
        return carry

    lax.fori_loop(0, XG, smooth_z, 0)

    def smooth_x(x, carry):
        total = None
        for k in range(2 * RADIUS + 1):
            term = weights[k] * zs[pl.ds(pl.multiple_of((x + k) * Y, 8), Y), :]
            total = term if total is None else total + term
        gx[pl.ds(pl.multiple_of(x * Y, 8), Y), :] = total
        return carry

    lax.fori_loop(0, XE, smooth_x, 0)

    def fold_g(y, carry):
        for r in range(R):
            gext[GHALO + y, pl.ds(8 * r, 8), :] = gx[pl.ds(r * Y + y, 8, stride=R * Y), :]
        return carry

    lax.fori_loop(0, Y, fold_g, 0)

    def to_wide(src, dst, k, target):
        return pltpu.make_async_remote_copy(
            src_ref=src, dst_ref=dst, send_sem=ys_sem.at[k], recv_sem=yr_sem.at[k],
            device_id=(target, narrow), device_id_type=MESH,
        )

    ysends = [
        to_wide(gext.at[pl.ds(Y, GHALO)], gext.at[pl.ds(0, GHALO)], 0, up),
        to_wide(gext.at[pl.ds(GHALO, GHALO)], gext.at[pl.ds(Y + GHALO, GHALO)], 1, down),
        to_wide(fld.at[:, pl.ds(Y, HALO)], fld.at[:, pl.ds(0, HALO)], 2, up),
        to_wide(fld.at[:, pl.ds(HALO, HALO)], fld.at[:, pl.ds(Y + HALO, HALO)], 3, down),
    ]
    ysends[0].start()
    ysends[1].start()

    own[1].wait()
    own[2].wait()
    for k in (1, 2, 4, 5):
        xsends[k].wait_recv()

    def fold_f(y, carry):
        for q in range(4):
            for r in range(R):
                fld[q, HALO + y, pl.ds(8 * r, 8), :] = nat[q, pl.ds(r * Y + y, 8, stride=R * Y), :]
        return carry

    lax.fori_loop(0, Y, fold_f, 0)
    ysends[2].start()
    ysends[3].start()

    def over_rows(spans, row_fn):
        (first, last) = spans[0]
        if len(spans) == 1:
            lax.fori_loop(first, last, lambda y, c: (row_fn(y), c)[1], 0)
        else:
            gap = spans[1][0] - last

            def step(i, c):
                row_fn(jnp.where(i < last, i, i + gap))
                return c

            lax.fori_loop(first, last + spans[1][1] - spans[1][0], step, 0)

    def first_row(y):
        for r in range(R):
            at = pl.ds(8 * r, 8)
            g = weights[RADIUS] * gext[y + RADIUS, at, :]
            for k in range(1, RADIUS + 1):
                g = g + weights[RADIUS + k] * (
                    gext[y + RADIUS - k, at, :] + gext[y + RADIUS + k, at, :])
            grey[y, at, :] = g
            rho = fld[0, y, at, :]
            u = [fld[1 + n, y, at, :] for n in range(3)]
            v = [1.5 * part for part in u]
            rho12 = rho * (1.0 / 12.0)
            j = [rho12 * part for part in u]
            flip = 1.0 - 2.0 * g
            w = [flip * part for part in j]
            usq = u[0] * v[0] + u[1] * v[1] + u[2] * v[2]
            base = (rho * (1.0 / 36.0)) * (1.0 - usq)
            fa[0, y, at, :] = 12.0 * base
            base2 = base + base
            for i in range(1, 19, 2):
                even = dot_c(i, j) * dot_c(i, v)
                odd = dot_c(i, w)
                if i < 7:
                    even = base2 + (even + even)
                    odd = odd + odd
                else:
                    even = base + even
                fa[i, y, at, :] = even + odd
                fa[i + 1, y, at, :] = even - odd

    def pulled(old, y, r):
        fields = []
        for cx, cy, cz in VELOCITIES:
            i = len(fields)
            rr = r - cx
            turn = 0
            if rr < 0:
                rr, turn = R - 1, 1
            elif rr == R:
                rr, turn = 0, 7
            f = old[i, y - cy, pl.ds(8 * rr, 8), :]
            if turn:
                f = pltpu.roll(f, turn, 0)
            if cz:
                f = pltpu.roll(f, cz % f.shape[1], 1)
            fields.append(f)
        return fields

    def collide_row(old, new, y):
        for r in range(R):
            at = pl.ds(8 * r, 8)
            fields = pulled(old, y, r)
            rho, m, sums, diffs = sums_and_differences(fields)
            g = grey[y, at, :]
            om = 1.0 - g
            b = 1.25 * om
            a = -0.25 * om
            apg = a + g
            ca = 0.5 * apg
            cb = 0.5 * (a - g)
            inv = 1.5 / rho
            v = [inv * part for part in m]
            b12 = b * (1.0 / 12.0)
            j = [b12 * part for part in m]
            vsq = v[0] * v[0] + v[1] * v[1] + v[2] * v[2]
            base = ((b * (1.0 / 36.0)) * rho) * (1.0 - (2.0 / 3.0) * vsq)
            new[0, y, at, :] = apg * fields[0] + 12.0 * base
            base2 = base + base
            for p, i in enumerate(range(1, 19, 2)):
                odd = dot_c(i, j)
                even = odd * dot_c(i, v)
                if i < 7:
                    even = base2 + (even + even)
                    odd = odd + odd
                else:
                    even = base + even
                even = ca * sums[p] + even
                odd = cb * diffs[p] + odd
                new[i, y, at, :] = even + odd
                new[i + 1, y, at, :] = even - odd

    def final_row(old, y):
        for r in range(R):
            rho, m, _, _ = sums_and_differences(pulled(old, y, r))
            at = pl.ds(r * Y + y - HALO, 8, stride=R * Y)
            mom[0, at, :] = rho
            for n in range(3):
                mom[1 + n, at, :] = m[n]

    bufs = (fa, fb)
    over_rows([(HALO + RADIUS, Y + HALO - RADIUS)], first_row)
    for t in range(1, STEPS):
        over_rows(
            [(HALO + RADIUS + t, Y + HALO - RADIUS - t)],
            functools.partial(collide_row, bufs[(t - 1) % 2], bufs[t % 2]),
        )
    for copy in ysends:
        copy.wait_recv()
    over_rows([(0, HALO + RADIUS), (YE - HALO - RADIUS, YE)], first_row)
    for t in range(1, STEPS):
        over_rows(
            [(t, HALO + RADIUS + t), (YE - HALO - RADIUS - t, YE - t)],
            functools.partial(collide_row, bufs[(t - 1) % 2], bufs[t % 2]),
        )
    over_rows([(HALO, Y + HALO)], functools.partial(final_row, bufs[(STEPS - 1) % 2]))

    sub = lax.broadcasted_iota(jnp.int32, (8, 128), 0)
    grp = lax.broadcasted_iota(jnp.int32, (8, 128), 1) // BS
    same = [((sub // b) % 2) == ((grp // b) % 2) for b in (1, 2, 4)]
    low = [((sub // b) % 2) == 0 for b in (1, 2, 4)]

    def swap(v):
        for n, b in enumerate((1, 2, 4)):
            ahead = pltpu.roll(pltpu.roll(v, 8 - b, 0), BS * b, 1)
            if b == 4:
                other = ahead
            else:
                back = pltpu.roll(pltpu.roll(v, b, 0), 128 - BS * b, 1)
                other = jnp.where(low[n], ahead, back)
            v = jnp.where(same[n], v, other)
        return v

    halves = Y // 8
    chunks = BS * halves

    def to_rows(a, carry):
        for bx in range(X // BS):
            for h in range(halves):
                for q in range(4):
                    v = mom[q, pl.ds(pl.multiple_of((HALO + bx * BS + a) * Y + 8 * h, 8), 8), :]
                    rows[pl.ds(8 * bx * 4 * chunks + q * chunks + a * halves + h, 8,
                               stride=4 * chunks), :] = swap(v)
        return carry

    lax.fori_loop(0, BS, to_rows, 0)

    per = 4 * chunks
    blocks = (X // BS) * 8
    keep = pltpu.make_async_copy(rows, src_out.at[pl.ds(0, blocks * per)], out_sem)
    keep.start()
    sends = []
    for offset in range(1, wide_count):
        target = lax.rem(wide + offset, wide_count)
        for k in range(2):
            j = mail_src[target * 2 + k]
            mail[pl.ds((2 * offset + k) * per, per), :] = rows[pl.ds(j * per, per), :]
        copy = pltpu.make_async_remote_copy(
            src_ref=mail.at[pl.ds(2 * offset * per, 2 * per)],
            dst_ref=src_out.at[pl.ds((blocks + 2 * wide) * per, 2 * per)],
            send_sem=as_sem.at[offset - 1], recv_sem=ar_sem.at[offset - 1],
            device_id=(target, narrow), device_id_type=MESH,
        )
        copy.start()
        sends.append(copy)
    for copy in xsends + ysends:
        copy.wait_send()
    keep.wait()
    for copy in sends:
        copy.wait()


def collect_kernel(rows_of, src, out):
    per = 4 * out.shape[2] // 8
    count = src.shape[0] // per
    chunks = out.shape[2] // 8

    def group(sg, carry):
        for si in range(8):
            row = rows_of[sg * 8 + si]
            there = row < count
            at = jnp.minimum(row, count - 1) * per
            for q in range(4):
                for k in range(chunks // 8):
                    v = src[pl.ds(pl.multiple_of(at + q * chunks + 8 * k, 8), 8), :]
                    out[q, sg, pl.ds(64 * k + si, 8, stride=8), :] = jnp.where(there, v, 0.0)
        return carry

    lax.fori_loop(0, out.shape[1], group, 0)


def routing(owner_map, my_index):
    blocks_x, wide_count, blocks_z = owner_map.shape
    block_count = blocks_x * blocks_z
    capacity = block_count + 2 * (wide_count - 1) - 2 * ((wide_count - 1) // 2)
    places = jnp.arange(block_count, dtype=jnp.int32)
    mine = lax.dynamic_index_in_dim(owner_map, my_index, 1, keepdims=False).reshape(block_count)
    rank = jnp.sum(
        (mine[:, None] == mine[None, :]) & (places[None, :] < places[:, None]), axis=1)
    slots = jnp.arange(2 * wide_count, dtype=jnp.int32)
    mail_src = jnp.sum(
        jnp.where((mine * 2 + rank)[None, :] == slots[:, None], places[None, :], 0)
        * (rank < 2)[None, :].astype(jnp.int32), axis=1)
    mail_src = jnp.minimum(mail_src, block_count - 1)
    here = (owner_map == my_index).astype(jnp.int32)
    counts = jnp.sum(here, axis=(0, 2))
    homes = slots // 2
    from_mail = (counts[homes] > slots % 2) & (homes != my_index)
    flags = jnp.concatenate([mine == my_index, from_mail])
    order = jnp.arange(flags.shape[0], dtype=jnp.int32)
    position = jnp.sum(flags[None, :] & (order[None, :] < order[:, None]), axis=1)
    wanted = jnp.arange(capacity, dtype=jnp.int32)
    hit = flags[None, :] & (position[None, :] == wanted[:, None])
    rows_of = jnp.sum(jnp.where(hit, order[None, :] + 1, 0), axis=1) - 1
    rows_of = jnp.where(rows_of < 0, flags.shape[0], rows_of)
    return mail_src.astype(jnp.int32), rows_of.astype(jnp.int32), capacity


def body(wide_count, narrow_count, labels, density, velocity, owner_map):
    X, Y, Z = labels.shape
    my_index = lax.axis_index("wide")
    mail_src, rows_of, capacity = routing(owner_map, my_index)
    XE, YE = X + 2 * HALO, Y + 2 * HALO
    XG, YG = X + 2 * GHALO, Y + 2 * GHALO
    blocks = (X // BS) * (Z // BS)
    chunks = BS * BS * BS // 128
    per = 4 * chunks
    f32 = jnp.float32
    hbm = pl.BlockSpec(memory_space=pl.ANY)
    src = pl.pallas_call(
        functools.partial(flow_kernel, wide_count, narrow_count, X, Y),
        out_shape=jax.ShapeDtypeStruct(((blocks + 2 * wide_count) * per, Z), f32),
        in_specs=[hbm, hbm, hbm, pl.BlockSpec(memory_space=pltpu.SMEM)],
        out_specs=hbm,
        scratch_shapes=[
            pltpu.VMEM((4, XE * Y, Z), f32),
            pltpu.VMEM((XG * Y, Z), jnp.int32),
            pltpu.VMEM((XG * Y, Z), f32),
            pltpu.VMEM((XE * Y, Z), f32),
            pltpu.VMEM((4, YE, XE, Z), f32),
            pltpu.VMEM((YG, XE, Z), f32),
            pltpu.VMEM((YE, XE, Z), f32),
            pltpu.VMEM((19, YE, XE, Z), f32),
            pltpu.VMEM((19, YE, XE, Z), f32),
            pltpu.VMEM((4, XE * Y, Z), f32),
            pltpu.VMEM((blocks * per, Z), f32),
            pltpu.VMEM((2 * wide_count * per, Z), f32),
            pltpu.SemaphoreType.DMA((3,)),
            pltpu.SemaphoreType.DMA((6,)),
            pltpu.SemaphoreType.DMA((6,)),
            pltpu.SemaphoreType.DMA((4,)),
            pltpu.SemaphoreType.DMA((4,)),
            pltpu.SemaphoreType.DMA((wide_count - 1,)),
            pltpu.SemaphoreType.DMA((wide_count - 1,)),
            pltpu.SemaphoreType.DMA,
        ],
        compiler_params=pltpu.CompilerParams(
            collective_id=0, has_side_effects=True, vmem_limit_bytes=60 * 1024 * 1024
        ),
        name="flow",
    )(labels.reshape(X * Y, Z), density.reshape(1, X * Y, Z), velocity.reshape(3, X * Y, Z), mail_src)
    groups = capacity // 8
    out = pl.pallas_call(
        collect_kernel,
        out_shape=jax.ShapeDtypeStruct((4, groups, chunks * 8, Z), f32),
        in_specs=[
            pl.BlockSpec(memory_space=pltpu.SMEM),
            pl.BlockSpec(memory_space=pltpu.VMEM),
        ],
        out_specs=pl.BlockSpec(memory_space=pltpu.VMEM),
        compiler_params=pltpu.CompilerParams(vmem_limit_bytes=48 * 1024 * 1024),
        name="collect",
    )(rows_of, src)
    out = out.reshape(4, groups, chunks, 8, Z).transpose(0, 1, 3, 2, 4)
    return out.reshape(4, 1, 1, capacity, BS * BS * BS)


def solution(mesh):
    placed = (
        P("narrow", "wide", None),
        P("narrow", "wide", None),
        P(None, "narrow", "wide", None),
        P("narrow", None, None),
    )
    return jax.shard_map(
        functools.partial(body, mesh.shape["wide"], mesh.shape["narrow"]),
        mesh=mesh,
        in_specs=placed,
        out_specs=P(None, "narrow", "wide", None, None),
        check_vma=False,
    )
```

```python
import functools
import math

import jax
import jax.numpy as jnp
from jax import lax
from jax.experimental import pallas as pl
from jax.experimental.pallas import tpu as pltpu
from jax.sharding import PartitionSpec as P

BS = 16
RADIUS = 2
STEPS = 4
HALO = STEPS
GHALO = HALO + RADIUS
YHALO = 1
YGHALO = YHALO + RADIUS

VELOCITIES = (
    (0, 0, 0),
    (1, 0, 0),
    (-1, 0, 0),
    (0, 1, 0),
    (0, -1, 0),
    (0, 0, 1),
    (0, 0, -1),
    (1, 1, 0),
    (-1, -1, 0),
    (1, -1, 0),
    (-1, 1, 0),
    (1, 0, 1),
    (-1, 0, -1),
    (1, 0, -1),
    (-1, 0, 1),
    (0, 1, 1),
    (0, -1, -1),
    (0, 1, -1),
    (0, -1, 1),
)
MESH = pl.DeviceIdType.MESH
UPWARD = [i for i in range(19) if VELOCITIES[i][1] > 0]
DOWNWARD = [i for i in range(19) if VELOCITIES[i][1] < 0]
ORDER = UPWARD + DOWNWARD + [i for i in range(19) if VELOCITIES[i][1] == 0]
SLOT = [ORDER.index(i) for i in range(19)]
CROSS = len(UPWARD)


def gauss_weights(radius):
    raw_values = [math.exp(-0.5 * offset * offset) for offset in range(-radius, radius + 1)]
    running = 0.0
    for element in raw_values:
        running = running + element
    return [element / running for element in raw_values]


def dot_c(direction, parts):
    running = None
    for sign, part in zip(VELOCITIES[direction], parts):
        if sign == 0:
            continue
        if running is None:
            running = part if sign > 0 else -part
        else:
            running = running + part if sign > 0 else running - part
    return running


def sums_and_differences(fields):
    sums, diffs = [], []
    mom = [None, None, None]
    rho = fields[0]
    for i in range(1, 19, 2):
        s = fields[i] + fields[i + 1]
        d = fields[i] - fields[i + 1]
        sums.append(s)
        diffs.append(d)
        rho = rho + s
        for axis_no in range(3):
            sign = VELOCITIES[i][axis_no]
            if sign != 0:
                if mom[axis_no] is None:
                    mom[axis_no] = d if sign > 0 else -d
                else:
                    mom[axis_no] = mom[axis_no] + d if sign > 0 else mom[axis_no] - d
    return rho, mom, sums, diffs


def flow_kernel(
    wide_count, narrow_count, X, Y,
    labels, density, velocity, mail_src,
    src_out,
    nat, natl, zs, gx, fld, gext, grey, fa, fb, mom, rows, mail,
    own_sem, xs_sem, xr_sem, ys_sem, yr_sem, ps_sem, pr_sem, as_sem, ar_sem, out_sem,
):
    weights = gauss_weights(RADIUS)
    XE = X + 2 * HALO
    XG = X + 2 * GHALO
    R = XE // 8
    lo, hi = YHALO, YHALO + Y - 1
    wide = lax.axis_index("wide")
    narrow = lax.axis_index("narrow")
    right = lax.rem(narrow + 1, narrow_count)
    left = lax.rem(narrow + narrow_count - 1, narrow_count)
    up = lax.rem(wide + 1, wide_count)
    down = lax.rem(wide + wide_count - 1, wide_count)

    own = [
        pltpu.make_async_copy(labels, natl.at[pl.ds(GHALO * Y, X * Y)], own_sem.at[0]),
        pltpu.make_async_copy(density, nat.at[pl.ds(0, 1), pl.ds(HALO * Y, X * Y)], own_sem.at[1]),
        pltpu.make_async_copy(velocity, nat.at[pl.ds(1, 3), pl.ds(HALO * Y, X * Y)], own_sem.at[2]),
    ]
    for copy in own:
        copy.start()

    barrier = pltpu.get_barrier_semaphore()
    for target in (left, right):
        pl.semaphore_signal(barrier, inc=1, device_id=(wide, target), device_id_type=MESH)
    for offset in range(1, wide_count):
        pl.semaphore_signal(
            barrier, inc=1, device_id=(lax.rem(wide + offset, wide_count), narrow),
            device_id_type=MESH,
        )
    pl.semaphore_wait(barrier, 2 + wide_count - 1)

    def to_narrow(src, dst, k, target):
        return pltpu.make_async_remote_copy(
            src_ref=src, dst_ref=dst, send_sem=xs_sem.at[k], recv_sem=xr_sem.at[k],
            device_id=(wide, target), device_id_type=MESH,
        )

    xsends = []
    for k, (target, at, to_g, to_f) in enumerate(
        ((right, X, 0, 0), (left, None, X + GHALO, X + HALO))
    ):
        g_at = (X - GHALO) * Y if at is not None else 0
        f_at = (X - HALO) * Y if at is not None else 0
        xsends.append(to_narrow(labels.at[pl.ds(g_at, GHALO * Y)],
                                natl.at[pl.ds(to_g * Y, GHALO * Y)], 3 * k, target))
        xsends.append(to_narrow(density.at[:, pl.ds(f_at, HALO * Y)],
                                nat.at[pl.ds(0, 1), pl.ds(to_f * Y, HALO * Y)], 3 * k + 1, target))
        xsends.append(to_narrow(velocity.at[:, pl.ds(f_at, HALO * Y)],
                                nat.at[pl.ds(1, 3), pl.ds(to_f * Y, HALO * Y)], 3 * k + 2, target))
    for copy in xsends:
        copy.start()

    def to_wide(src, dst, sems, k, target):
        return pltpu.make_async_remote_copy(
            src_ref=src, dst_ref=dst, send_sem=sems[0].at[k], recv_sem=sems[1].at[k],
            device_id=(target, narrow), device_id_type=MESH,
        )

    ysem = (ys_sem, yr_sem)
    ysends = [
        to_wide(fld.at[:, pl.ds(Y, YHALO)], fld.at[:, pl.ds(0, YHALO)], ysem, 0, up),
        to_wide(fld.at[:, pl.ds(lo, YHALO)], fld.at[:, pl.ds(Y + YHALO, YHALO)], ysem, 1, down),
        to_wide(gext.at[pl.ds(Y, YGHALO)], gext.at[pl.ds(0, YGHALO)], ysem, 2, up),
        to_wide(gext.at[pl.ds(YGHALO, YGHALO)], gext.at[pl.ds(Y + YGHALO, YGHALO)], ysem, 3, down),
    ]

    def smooth_z(x, carry):
        at = pl.ds(pl.multiple_of(x * Y, 8), Y)
        v = natl[at, :].astype(jnp.float32)
        total = weights[RADIUS] * v
        for k in range(1, RADIUS + 1):
            total = total + weights[RADIUS + k] * (
                pltpu.roll(v, k, 1) + pltpu.roll(v, v.shape[1] - k, 1))
        zs[at, :] = total
        return carry

    def smooth_x(x, carry):
        total = None
        for k in range(2 * RADIUS + 1):
            term = weights[k] * zs[pl.ds(pl.multiple_of((x + k) * Y, 8), Y), :]
            total = term if total is None else total + term
        gx[pl.ds(pl.multiple_of(x * Y, 8), Y), :] = total
        return carry

    def fold_g(y, carry):
        for r in range(R):
            gext[YGHALO + y, pl.ds(8 * r, 8), :] = gx[pl.ds(r * Y + y, 8, stride=R * Y), :]
        return carry

    def fold_f(y, carry):
        for q in range(4):
            for r in range(R):
                fld[q, lo + y, pl.ds(8 * r, 8), :] = nat[q, pl.ds(r * Y + y, 8, stride=R * Y), :]
        return carry

    own[0].wait()
    lax.fori_loop(GHALO, GHALO + X, smooth_z, 0)
    own[1].wait()
    own[2].wait()
    for k in (1, 2, 4, 5):
        xsends[k].wait_recv()
    fold_f(0, 0)
    fold_f(Y - 1, 0)
    ysends[0].start()
    ysends[1].start()
    xsends[0].wait_recv()
    xsends[3].wait_recv()
    lax.fori_loop(0, GHALO, smooth_z, 0)
    lax.fori_loop(GHALO + X, XG, smooth_z, 0)
    lax.fori_loop(0, XE, smooth_x, 0)
    lax.fori_loop(0, Y, fold_g, 0)
    ysends[2].start()
    ysends[3].start()
    lax.fori_loop(1, Y - 1, fold_f, 0)

    def over_rows(spans, row_fn):
        (first, last) = spans[0]
        if len(spans) == 1:
            lax.fori_loop(first, last, lambda y, c: (row_fn(y), c)[1], 0)
        else:
            gap = spans[1][0] - last

            def step(i, c):
                row_fn(jnp.where(i < last, i, i + gap))
                return c

            lax.fori_loop(first, last + spans[1][1] - spans[1][0], step, 0)

    def first_row(y):
        for r in range(R):
            at = pl.ds(8 * r, 8)
            g = weights[RADIUS] * gext[y + RADIUS, at, :]
            for k in range(1, RADIUS + 1):
                g = g + weights[RADIUS + k] * (
                    gext[y + RADIUS - k, at, :] + gext[y + RADIUS + k, at, :])
            grey[y, at, :] = g
            rho = fld[0, y, at, :]
            u = [fld[1 + n, y, at, :] for n in range(3)]
            v = [1.5 * part for part in u]
            rho12 = rho * (1.0 / 12.0)
            j = [rho12 * part for part in u]
            flip = 1.0 - 2.0 * g
            w = [flip * part for part in j]
            usq = u[0] * v[0] + u[1] * v[1] + u[2] * v[2]
            base = (rho * (1.0 / 36.0)) * (1.0 - usq)
            fa[SLOT[0], y, at, :] = 12.0 * base
            base2 = base + base
            for i in range(1, 19, 2):
                even = dot_c(i, j) * dot_c(i, v)
                odd = dot_c(i, w)
                if i < 7:
                    even = base2 + (even + even)
                    odd = odd + odd
                else:
                    even = base + even
                fa[SLOT[i], y, at, :] = even + odd
                fa[SLOT[i + 1], y, at, :] = even - odd

    def pulled(old, y, r):
        fields = []
        for cx, cy, cz in VELOCITIES:
            i = len(fields)
            rr = r - cx
            turn = 0
            if rr < 0:
                rr, turn = R - 1, 1
            elif rr == R:
                rr, turn = 0, 7
            f = old[SLOT[i], y - cy, pl.ds(8 * rr, 8), :]
            if turn:
                f = pltpu.roll(f, turn, 0)
            if cz:
                f = pltpu.roll(f, cz % f.shape[1], 1)
            fields.append(f)
        return fields

    def collide_row(old, new, y):
        for r in range(R):
            at = pl.ds(8 * r, 8)
            fields = pulled(old, y, r)
            rho, m, sums, diffs = sums_and_differences(fields)
            g = grey[y, at, :]
            om = 1.0 - g
            b = 1.25 * om
            a = -0.25 * om
            apg = a + g
            ca = 0.5 * apg
            cb = 0.5 * (a - g)
            inv = 1.5 / rho
            v = [inv * part for part in m]
            b12 = b * (1.0 / 12.0)
            j = [b12 * part for part in m]
            vsq = v[0] * v[0] + v[1] * v[1] + v[2] * v[2]
            base = ((b * (1.0 / 36.0)) * rho) * (1.0 - (2.0 / 3.0) * vsq)
            new[SLOT[0], y, at, :] = apg * fields[0] + 12.0 * base
            base2 = base + base
            for p, i in enumerate(range(1, 19, 2)):
                odd = dot_c(i, j)
                even = odd * dot_c(i, v)
                if i < 7:
                    even = base2 + (even + even)
                    odd = odd + odd
                else:
                    even = base + even
                even = ca * sums[p] + even
                odd = cb * diffs[p] + odd
                new[SLOT[i], y, at, :] = even + odd
                new[SLOT[i + 1], y, at, :] = even - odd

    def final_row(old, y):
        for r in range(R):
            rho, m, _, _ = sums_and_differences(pulled(old, y, r))
            at = pl.ds(r * Y + y - lo, 8, stride=R * Y)
            mom[0, at, :] = rho
            for n in range(3):
                mom[1 + n, at, :] = m[n]

    def trade(buf, t):
        sem = (ps_sem, pr_sem)
        return [
            to_wide(buf.at[pl.ds(0, CROSS), hi], buf.at[pl.ds(0, CROSS), lo - 1], sem, 2 * t, up),
            to_wide(buf.at[pl.ds(CROSS, CROSS), lo], buf.at[pl.ds(CROSS, CROSS), hi + 1], sem,
                    2 * t + 1, down),
        ]

    step_a = functools.partial(collide_row, fa, fb)
    over_rows([(lo + RADIUS, hi + 1 - RADIUS)], first_row)
    over_rows([(lo + RADIUS + 1, hi - RADIUS)], step_a)
    for copy in ysends:
        copy.wait_recv()
    over_rows([(lo - 1, lo + RADIUS), (hi + 1 - RADIUS, hi + 2)], first_row)
    psends = []
    for t in range(STEPS):
        old, new = ((fa, fb), (fb, fa))[t % 2]
        if t > 0:
            for copy in psends[-1]:
                copy.wait_recv()
        if t < STEPS - 1:
            if t > 1:
                for copy in psends[-2]:
                    copy.wait_send()
            over_rows([(lo, lo + 1), (hi, hi + 1)], functools.partial(collide_row, old, new))
            psends.append(trade(new, t))
            for copy in psends[-1]:
                copy.start()
            if t == 0:
                over_rows([(lo + 1, lo + RADIUS + 1), (hi - RADIUS, hi)], step_a)
            if t < STEPS - 2:
                over_rows([(lo + 1, hi)], functools.partial(collide_row, new, old))
            else:
                over_rows([(lo + 1, hi)], functools.partial(final_row, new))
        else:
            over_rows([(lo, lo + 1), (hi, hi + 1)], functools.partial(final_row, old))

    sub = lax.broadcasted_iota(jnp.int32, (8, 128), 0)
    grp = lax.broadcasted_iota(jnp.int32, (8, 128), 1) // BS
    same = [((sub // b) % 2) == ((grp // b) % 2) for b in (1, 2, 4)]
    low = [((sub // b) % 2) == 0 for b in (1, 2, 4)]

    def swap(v):
        for n, b in enumerate((1, 2, 4)):
            ahead = pltpu.roll(pltpu.roll(v, 8 - b, 0), BS * b, 1)
            if b == 4:
                other = ahead
            else:
                back = pltpu.roll(pltpu.roll(v, b, 0), 128 - BS * b, 1)
                other = jnp.where(low[n], ahead, back)
            v = jnp.where(same[n], v, other)
        return v

    halves = Y // 8
    chunks = BS * halves

    def to_rows(a, carry):
        for bx in range(X // BS):
            for h in range(halves):
                for q in range(4):
                    v = mom[q, pl.ds(pl.multiple_of((HALO + bx * BS + a) * Y + 8 * h, 8), 8), :]
                    rows[pl.ds(8 * bx * 4 * chunks + q * chunks + a * halves + h, 8,
                               stride=4 * chunks), :] = swap(v)
        return carry

    lax.fori_loop(0, BS, to_rows, 0)

    per = 4 * chunks
    blocks = (X // BS) * 8
    keep = pltpu.make_async_copy(rows, src_out.at[pl.ds(0, blocks * per)], out_sem)
    keep.start()
    sends = []
    for offset in range(1, wide_count):
        target = lax.rem(wide + offset, wide_count)
        for k in range(2):
            j = mail_src[target * 2 + k]
            mail[pl.ds((2 * offset + k) * per, per), :] = rows[pl.ds(j * per, per), :]
        copy = pltpu.make_async_remote_copy(
            src_ref=mail.at[pl.ds(2 * offset * per, 2 * per)],
            dst_ref=src_out.at[pl.ds((blocks + 2 * wide) * per, 2 * per)],
            send_sem=as_sem.at[offset - 1], recv_sem=ar_sem.at[offset - 1],
            device_id=(target, narrow), device_id_type=MESH,
        )
        copy.start()
        sends.append(copy)
    for copy in xsends + ysends + psends[-2] + psends[-1]:
        copy.wait_send()
    keep.wait()
    for copy in sends:
        copy.wait()


def collect_kernel(rows_of, src, out):
    count, _, chunks, _ = src.shape

    def group(sg, carry):
        for si in range(8):
            row = rows_of[sg * 8 + si]
            there = row < count
            at = jnp.minimum(row, count - 1)
            for k in range(chunks // 8):
                v = src[at, 0, pl.ds(8 * k, 8), :]
                out[0, sg, pl.ds(64 * k + si, 8, stride=8), :] = jnp.where(there, v, 0.0)
        return carry

    lax.fori_loop(0, out.shape[1], group, 0)


def routing(owner_map, my_index):
    blocks_x, wide_count, blocks_z = owner_map.shape
    block_count = blocks_x * blocks_z
    capacity = block_count + 2 * (wide_count - 1) - 2 * ((wide_count - 1) // 2)
    places = jnp.arange(block_count, dtype=jnp.int32)
    mine = lax.dynamic_index_in_dim(owner_map, my_index, 1, keepdims=False).reshape(block_count)
    rank = jnp.sum(
        (mine[:, None] == mine[None, :]) & (places[None, :] < places[:, None]), axis=1)
    slots = jnp.arange(2 * wide_count, dtype=jnp.int32)
    mail_src = jnp.sum(
        jnp.where((mine * 2 + rank)[None, :] == slots[:, None], places[None, :], 0)
        * (rank < 2)[None, :].astype(jnp.int32), axis=1)
    mail_src = jnp.minimum(mail_src, block_count - 1)
    here = (owner_map == my_index).astype(jnp.int32)
    counts = jnp.sum(here, axis=(0, 2))
    homes = slots // 2
    from_mail = (counts[homes] > slots % 2) & (homes != my_index)
    flags = jnp.concatenate([mine == my_index, from_mail])
    order = jnp.arange(flags.shape[0], dtype=jnp.int32)
    position = jnp.sum(flags[None, :] & (order[None, :] < order[:, None]), axis=1)
    wanted = jnp.arange(capacity, dtype=jnp.int32)
    hit = flags[None, :] & (position[None, :] == wanted[:, None])
    rows_of = jnp.sum(jnp.where(hit, order[None, :] + 1, 0), axis=1) - 1
    rows_of = jnp.where(rows_of < 0, flags.shape[0], rows_of)
    return mail_src.astype(jnp.int32), rows_of.astype(jnp.int32), capacity


def body(wide_count, narrow_count, labels, density, velocity, owner_map):
    X, Y, Z = labels.shape
    my_index = lax.axis_index("wide")
    mail_src, rows_of, capacity = routing(owner_map, my_index)
    XE, YE = X + 2 * HALO, Y + 2 * YHALO
    XG, YG = X + 2 * GHALO, Y + 2 * YGHALO
    blocks = (X // BS) * (Z // BS)
    chunks = BS * BS * BS // 128
    per = 4 * chunks
    f32 = jnp.float32
    hbm = pl.BlockSpec(memory_space=pl.ANY)
    src = pl.pallas_call(
        functools.partial(flow_kernel, wide_count, narrow_count, X, Y),
        out_shape=jax.ShapeDtypeStruct(((blocks + 2 * wide_count) * per, Z), f32),
        in_specs=[hbm, hbm, hbm, pl.BlockSpec(memory_space=pltpu.SMEM)],
        out_specs=hbm,
        scratch_shapes=[
            pltpu.VMEM((4, XE * Y, Z), f32),
            pltpu.VMEM((XG * Y, Z), jnp.int32),
            pltpu.VMEM((XG * Y, Z), f32),
            pltpu.VMEM((XE * Y, Z), f32),
            pltpu.VMEM((4, YE, XE, Z), f32),
            pltpu.VMEM((YG, XE, Z), f32),
            pltpu.VMEM((YE, XE, Z), f32),
            pltpu.VMEM((19, YE, XE, Z), f32),
            pltpu.VMEM((19, YE, XE, Z), f32),
            pltpu.VMEM((4, XE * Y, Z), f32),
            pltpu.VMEM((blocks * per, Z), f32),
            pltpu.VMEM((2 * wide_count * per, Z), f32),
            pltpu.SemaphoreType.DMA((3,)),
            pltpu.SemaphoreType.DMA((6,)),
            pltpu.SemaphoreType.DMA((6,)),
            pltpu.SemaphoreType.DMA((4,)),
            pltpu.SemaphoreType.DMA((4,)),
            pltpu.SemaphoreType.DMA((2 * (STEPS - 1),)),
            pltpu.SemaphoreType.DMA((2 * (STEPS - 1),)),
            pltpu.SemaphoreType.DMA((wide_count - 1,)),
            pltpu.SemaphoreType.DMA((wide_count - 1,)),
            pltpu.SemaphoreType.DMA,
        ],
        compiler_params=pltpu.CompilerParams(
            collective_id=0, has_side_effects=True, vmem_limit_bytes=60 * 1024 * 1024
        ),
        name="flow",
    )(labels.reshape(X * Y, Z), density.reshape(1, X * Y, Z), velocity.reshape(3, X * Y, Z), mail_src)
    groups = capacity // 8
    out = pl.pallas_call(
        collect_kernel,
        out_shape=jax.ShapeDtypeStruct((4, groups, chunks * 8, Z), f32),
        grid=(4,),
        in_specs=[
            pl.BlockSpec(memory_space=pltpu.SMEM),
            pl.BlockSpec((blocks + 2 * wide_count, 1, chunks, Z), lambda q: (0, q, 0, 0)),
        ],
        out_specs=pl.BlockSpec((1, groups, chunks * 8, Z), lambda q: (q, 0, 0, 0)),
        compiler_params=pltpu.CompilerParams(vmem_limit_bytes=48 * 1024 * 1024),
        name="collect",
    )(rows_of, src.reshape(blocks + 2 * wide_count, 4, chunks, Z))
    out = out.reshape(4, groups, chunks, 8, Z).transpose(0, 1, 3, 2, 4)
    return out.reshape(4, 1, 1, capacity, BS * BS * BS)


def solution(mesh):
    placed = (
        P("narrow", "wide", None),
        P("narrow", "wide", None),
        P(None, "narrow", "wide", None),
        P("narrow", None, None),
    )
    return jax.shard_map(
        functools.partial(body, mesh.shape["wide"], mesh.shape["narrow"]),
        mesh=mesh,
        in_specs=placed,
        out_specs=P(None, "narrow", "wide", None, None),
        check_vma=False,
    )
```

```python
import functools
import math

import jax
import jax.numpy as jnp
from jax import lax
from jax.experimental import pallas as pl
from jax.experimental.pallas import tpu as pltpu
from jax.sharding import PartitionSpec as P

BS = 16
RADIUS = 2
STEPS = 4
HALO = STEPS
GHALO = HALO + RADIUS
YHALO = 1
YGHALO = YHALO + RADIUS

VELOCITIES = (
    (0, 0, 0),
    (1, 0, 0),
    (-1, 0, 0),
    (0, 1, 0),
    (0, -1, 0),
    (0, 0, 1),
    (0, 0, -1),
    (1, 1, 0),
    (-1, -1, 0),
    (1, -1, 0),
    (-1, 1, 0),
    (1, 0, 1),
    (-1, 0, -1),
    (1, 0, -1),
    (-1, 0, 1),
    (0, 1, 1),
    (0, -1, -1),
    (0, 1, -1),
    (0, -1, 1),
)
MESH = pl.DeviceIdType.MESH
UPWARD = [i for i in range(19) if VELOCITIES[i][1] > 0]
DOWNWARD = [i for i in range(19) if VELOCITIES[i][1] < 0]
ORDER = UPWARD + DOWNWARD + [i for i in range(19) if VELOCITIES[i][1] == 0]
SLOT = [ORDER.index(i) for i in range(19)]
CROSS = len(UPWARD)


def gauss_weights(radius):
    raw_values = [math.exp(-0.5 * offset * offset) for offset in range(-radius, radius + 1)]
    running = 0.0
    for element in raw_values:
        running = running + element
    return [element / running for element in raw_values]


def dot_c(direction, parts):
    running = None
    for sign, part in zip(VELOCITIES[direction], parts):
        if sign == 0:
            continue
        if running is None:
            running = part if sign > 0 else -part
        else:
            running = running + part if sign > 0 else running - part
    return running


def sums_and_differences(fields):
    sums, diffs = [], []
    mom = [None, None, None]
    rho = fields[0]
    for i in range(1, 19, 2):
        s = fields[i] + fields[i + 1]
        d = fields[i] - fields[i + 1]
        sums.append(s)
        diffs.append(d)
        rho = rho + s
        for axis_no in range(3):
            sign = VELOCITIES[i][axis_no]
            if sign != 0:
                if mom[axis_no] is None:
                    mom[axis_no] = d if sign > 0 else -d
                else:
                    mom[axis_no] = mom[axis_no] + d if sign > 0 else mom[axis_no] - d
    return rho, mom, sums, diffs


def flow_kernel(
    wide_count, narrow_count, X, Y,
    labels, density, velocity, mail_src,
    src_out,
    nat, natl, zs, gx, fld, gext, grey, fa, fb, mom, rows, mail,
    own_sem, xs_sem, xr_sem, ys_sem, yr_sem, ps_sem, pr_sem, as_sem, ar_sem, out_sem,
):
    weights = gauss_weights(RADIUS)
    XE = X + 2 * HALO
    XG = X + 2 * GHALO
    R = XE // 8
    lo, hi = YHALO, YHALO + Y - 1
    wide = lax.axis_index("wide")
    narrow = lax.axis_index("narrow")
    right = lax.rem(narrow + 1, narrow_count)
    left = lax.rem(narrow + narrow_count - 1, narrow_count)
    up = lax.rem(wide + 1, wide_count)
    down = lax.rem(wide + wide_count - 1, wide_count)

    own = [
        pltpu.make_async_copy(labels, natl.at[pl.ds(GHALO * Y, X * Y)], own_sem.at[0]),
        pltpu.make_async_copy(density, nat.at[pl.ds(0, 1), pl.ds(HALO * Y, X * Y)], own_sem.at[1]),
        pltpu.make_async_copy(velocity, nat.at[pl.ds(1, 3), pl.ds(HALO * Y, X * Y)], own_sem.at[2]),
    ]
    for copy in own:
        copy.start()

    barrier = pltpu.get_barrier_semaphore()
    for target in (left, right):
        pl.semaphore_signal(barrier, inc=1, device_id=(wide, target), device_id_type=MESH)
    for offset in range(1, wide_count):
        pl.semaphore_signal(
            barrier, inc=1, device_id=(lax.rem(wide + offset, wide_count), narrow),
            device_id_type=MESH,
        )
    pl.semaphore_wait(barrier, 2 + wide_count - 1)

    def to_narrow(src, dst, k, target):
        return pltpu.make_async_remote_copy(
            src_ref=src, dst_ref=dst, send_sem=xs_sem.at[k], recv_sem=xr_sem.at[k],
            device_id=(wide, target), device_id_type=MESH,
        )

    xsends = []
    for k, (target, at, to_g, to_f) in enumerate(
        ((right, X, 0, 0), (left, None, X + GHALO, X + HALO))
    ):
        g_at = (X - GHALO) * Y if at is not None else 0
        f_at = (X - HALO) * Y if at is not None else 0
        xsends.append(to_narrow(labels.at[pl.ds(g_at, GHALO * Y)],
                                natl.at[pl.ds(to_g * Y, GHALO * Y)], 3 * k, target))
        xsends.append(to_narrow(density.at[:, pl.ds(f_at, HALO * Y)],
                                nat.at[pl.ds(0, 1), pl.ds(to_f * Y, HALO * Y)], 3 * k + 1, target))
        xsends.append(to_narrow(velocity.at[:, pl.ds(f_at, HALO * Y)],
                                nat.at[pl.ds(1, 3), pl.ds(to_f * Y, HALO * Y)], 3 * k + 2, target))
    for copy in xsends:
        copy.start()

    def to_wide(src, dst, sems, k, target):
        return pltpu.make_async_remote_copy(
            src_ref=src, dst_ref=dst, send_sem=sems[0].at[k], recv_sem=sems[1].at[k],
            device_id=(target, narrow), device_id_type=MESH,
        )

    ysem = (ys_sem, yr_sem)
    ysends = [
        to_wide(fld.at[:, pl.ds(Y, YHALO)], fld.at[:, pl.ds(0, YHALO)], ysem, 0, up),
        to_wide(fld.at[:, pl.ds(lo, YHALO)], fld.at[:, pl.ds(Y + YHALO, YHALO)], ysem, 1, down),
        to_wide(gext.at[pl.ds(Y, YGHALO)], gext.at[pl.ds(0, YGHALO)], ysem, 2, up),
        to_wide(gext.at[pl.ds(YGHALO, YGHALO)], gext.at[pl.ds(Y + YGHALO, YGHALO)], ysem, 3, down),
    ]

    def smooth_z(x, count):
        at = pl.ds(pl.multiple_of(x * Y, 8), count * Y)
        v = natl[at, :].astype(jnp.float32)
        total = weights[RADIUS] * v
        for k in range(1, RADIUS + 1):
            total = total + weights[RADIUS + k] * (
                pltpu.roll(v, k, 1) + pltpu.roll(v, v.shape[1] - k, 1))
        zs[at, :] = total

    def smooth_x(x, count):
        total = None
        for k in range(2 * RADIUS + 1):
            term = weights[k] * zs[pl.ds(pl.multiple_of((x + k) * Y, 8), count * Y), :]
            total = term if total is None else total + term
        gx[pl.ds(pl.multiple_of(x * Y, 8), count * Y), :] = total

    def in_chunks(fn, first, count, size):
        def step(n, carry):
            fn(first + n * size, size)
            return carry

        lax.fori_loop(0, count // size, step, 0)

    def fold_g(y, carry):
        for r in range(R):
            gext[YGHALO + y, pl.ds(8 * r, 8), :] = gx[pl.ds(r * Y + y, 8, stride=R * Y), :]
        return carry

    def fold_f(y, carry):
        for q in range(4):
            for r in range(R):
                fld[q, lo + y, pl.ds(8 * r, 8), :] = nat[q, pl.ds(r * Y + y, 8, stride=R * Y), :]
        return carry

    own[0].wait()
    in_chunks(smooth_z, GHALO, X, 8)
    own[1].wait()
    own[2].wait()
    for k in (1, 2, 4, 5):
        xsends[k].wait_recv()
    fold_f(0, 0)
    fold_f(Y - 1, 0)
    ysends[0].start()
    ysends[1].start()
    xsends[0].wait_recv()
    xsends[3].wait_recv()
    smooth_z(0, GHALO)
    smooth_z(GHALO + X, GHALO)
    in_chunks(smooth_x, 0, XE, 4)
    lax.fori_loop(0, Y, fold_g, 0)
    ysends[2].start()
    ysends[3].start()
    lax.fori_loop(1, Y - 1, fold_f, 0)

    def over_rows(spans, row_fn):
        (first, last) = spans[0]
        if len(spans) == 1:
            lax.fori_loop(first, last, lambda y, c: (row_fn(y), c)[1], 0)
        else:
            gap = spans[1][0] - last

            def step(i, c):
                row_fn(jnp.where(i < last, i, i + gap))
                return c

            lax.fori_loop(first, last + spans[1][1] - spans[1][0], step, 0)

    def first_row(y):
        for r in range(R):
            at = pl.ds(8 * r, 8)
            g = weights[RADIUS] * gext[y + RADIUS, at, :]
            for k in range(1, RADIUS + 1):
                g = g + weights[RADIUS + k] * (
                    gext[y + RADIUS - k, at, :] + gext[y + RADIUS + k, at, :])
            grey[y, at, :] = g
            rho = fld[0, y, at, :]
            u = [fld[1 + n, y, at, :] for n in range(3)]
            v = [1.5 * part for part in u]
            rho12 = rho * (1.0 / 12.0)
            j = [rho12 * part for part in u]
            flip = 1.0 - 2.0 * g
            w = [flip * part for part in j]
            usq = u[0] * v[0] + u[1] * v[1] + u[2] * v[2]
            base = (rho * (1.0 / 36.0)) * (1.0 - usq)
            fa[SLOT[0], y, at, :] = 12.0 * base
            base2 = base + base
            for i in range(1, 19, 2):
                even = dot_c(i, j) * dot_c(i, v)
                odd = dot_c(i, w)
                if i < 7:
                    even = base2 + (even + even)
                    odd = odd + odd
                else:
                    even = base + even
                fa[SLOT[i], y, at, :] = even + odd
                fa[SLOT[i + 1], y, at, :] = even - odd

    def pulled(old, y, r):
        fields = []
        for cx, cy, cz in VELOCITIES:
            i = len(fields)
            rr = r - cx
            turn = 0
            if rr < 0:
                rr, turn = R - 1, 1
            elif rr == R:
                rr, turn = 0, 7
            f = old[SLOT[i], y - cy, pl.ds(8 * rr, 8), :]
            if turn:
                f = pltpu.roll(f, turn, 0)
            if cz:
                f = pltpu.roll(f, cz % f.shape[1], 1)
            fields.append(f)
        return fields

    def collide_row(old, new, y):
        for r in range(R):
            at = pl.ds(8 * r, 8)
            fields = pulled(old, y, r)
            rho, m, sums, diffs = sums_and_differences(fields)
            g = grey[y, at, :]
            om = 1.0 - g
            b = 1.25 * om
            a = -0.25 * om
            apg = a + g
            ca = 0.5 * apg
            cb = 0.5 * (a - g)
            inv = 1.5 / rho
            v = [inv * part for part in m]
            b12 = b * (1.0 / 12.0)
            j = [b12 * part for part in m]
            vsq = v[0] * v[0] + v[1] * v[1] + v[2] * v[2]
            base = ((b * (1.0 / 36.0)) * rho) * (1.0 - (2.0 / 3.0) * vsq)
            new[SLOT[0], y, at, :] = apg * fields[0] + 12.0 * base
            base2 = base + base
            for p, i in enumerate(range(1, 19, 2)):
                odd = dot_c(i, j)
                even = odd * dot_c(i, v)
                if i < 7:
                    even = base2 + (even + even)
                    odd = odd + odd
                else:
                    even = base + even
                even = ca * sums[p] + even
                odd = cb * diffs[p] + odd
                new[SLOT[i], y, at, :] = even + odd
                new[SLOT[i + 1], y, at, :] = even - odd

    def final_row(old, y):
        for r in range(R):
            rho, m, _, _ = sums_and_differences(pulled(old, y, r))
            at = pl.ds(r * Y + y - lo, 8, stride=R * Y)
            mom[0, at, :] = rho
            for n in range(3):
                mom[1 + n, at, :] = m[n]

    def trade(buf, t):
        sem = (ps_sem, pr_sem)
        return [
            to_wide(buf.at[pl.ds(0, CROSS), hi], buf.at[pl.ds(0, CROSS), lo - 1], sem, 2 * t, up),
            to_wide(buf.at[pl.ds(CROSS, CROSS), lo], buf.at[pl.ds(CROSS, CROSS), hi + 1], sem,
                    2 * t + 1, down),
        ]

    step_a = functools.partial(collide_row, fa, fb)
    over_rows([(lo + RADIUS, hi + 1 - RADIUS)], first_row)
    over_rows([(lo + RADIUS + 1, hi - RADIUS)], step_a)
    for copy in ysends:
        copy.wait_recv()
    over_rows([(lo - 1, lo + RADIUS), (hi + 1 - RADIUS, hi + 2)], first_row)
    psends = []
    for t in range(STEPS):
        old, new = ((fa, fb), (fb, fa))[t % 2]
        if t > 0:
            for copy in psends[-1]:
                copy.wait_recv()
        if t < STEPS - 1:
            if t > 1:
                for copy in psends[-2]:
                    copy.wait_send()
            over_rows([(lo, lo + 1), (hi, hi + 1)], functools.partial(collide_row, old, new))
            psends.append(trade(new, t))
            for copy in psends[-1]:
                copy.start()
            if t == 0:
                over_rows([(lo + 1, lo + RADIUS + 1), (hi - RADIUS, hi)], step_a)
            if t < STEPS - 2:
                over_rows([(lo + 1, hi)], functools.partial(collide_row, new, old))
            else:
                over_rows([(lo + 1, hi)], functools.partial(final_row, new))
        else:
            over_rows([(lo, lo + 1), (hi, hi + 1)], functools.partial(final_row, old))

    sub = lax.broadcasted_iota(jnp.int32, (8, 128), 0)
    grp = lax.broadcasted_iota(jnp.int32, (8, 128), 1) // BS
    same = [((sub // b) % 2) == ((grp // b) % 2) for b in (1, 2, 4)]
    low = [((sub // b) % 2) == 0 for b in (1, 2, 4)]

    def swap(v):
        for n, b in enumerate((1, 2, 4)):
            ahead = pltpu.roll(pltpu.roll(v, 8 - b, 0), BS * b, 1)
            if b == 4:
                other = ahead
            else:
                back = pltpu.roll(pltpu.roll(v, b, 0), 128 - BS * b, 1)
                other = jnp.where(low[n], ahead, back)
            v = jnp.where(same[n], v, other)
        return v

    halves = Y // 8
    chunks = BS * halves

    per = 4 * chunks
    blocks = (X // BS) * 8
    half = per // 2
    quarter = chunks // 2

    def to_rows(a, carry):
        part = a // (BS // 2)
        base = part * half + (a - part * (BS // 2)) * halves
        for bx in range(X // BS):
            for h in range(halves):
                for q in range(4):
                    v = mom[q, pl.ds(pl.multiple_of((HALO + bx * BS + a) * Y + 8 * h, 8), 8), :]
                    rows[pl.ds(8 * bx * per + base + q * quarter + h, 8, stride=per), :] = swap(v)
        return carry

    sends = []
    for part in range(2):
        lax.fori_loop(part * (BS // 2), (part + 1) * (BS // 2), to_rows, 0)
        for offset in range(1, wide_count):
            target = lax.rem(wide + offset, wide_count)
            for k in range(2):
                j = mail_src[target * 2 + k]
                here = pl.ds((2 * offset + k) * per + part * half, half)
                mail[here, :] = rows[pl.ds(j * per + part * half, half), :]
                n = 4 * (offset - 1) + 2 * part + k
                copy = pltpu.make_async_remote_copy(
                    src_ref=mail.at[here],
                    dst_ref=src_out.at[pl.ds((blocks + 2 * wide + k) * per + part * half, half)],
                    send_sem=as_sem.at[n], recv_sem=ar_sem.at[n],
                    device_id=(target, narrow), device_id_type=MESH,
                )
                copy.start()
                sends.append(copy)
    keep = pltpu.make_async_copy(rows, src_out.at[pl.ds(0, blocks * per)], out_sem)
    keep.start()
    for copy in xsends + ysends + psends[-2] + psends[-1]:
        copy.wait_send()
    keep.wait()
    for copy in sends:
        copy.wait()


def collect_kernel(rows_of, src, out):
    count, _, _, quarter, _ = src.shape

    def group(sg, carry):
        for si in range(8):
            row = rows_of[sg * 8 + si]
            there = row < count
            at = jnp.minimum(row, count - 1)
            for part in range(2):
                for k in range(quarter // 8):
                    v = src[at, part, 0, pl.ds(8 * k, 8), :]
                    out[0, sg, pl.ds(8 * (part * quarter + 8 * k) + si, 8, stride=8), :] = (
                        jnp.where(there, v, 0.0))
        return carry

    lax.fori_loop(0, out.shape[1], group, 0)


def routing_kernel(capacity, owners, mail_src, rows_of, seen):
    blocks_x, wide_count, blocks_z = owners.shape
    block_count = blocks_x * blocks_z
    me = lax.axis_index("wide")

    def clear(o, carry):
        seen[o] = 0
        mail_src[2 * o] = 0
        mail_src[2 * o + 1] = 0
        return carry

    lax.fori_loop(0, wide_count, clear, 0)
    slot = jnp.int32(0)
    for j in range(block_count):
        o = owners[j // blocks_z, me, j % blocks_z]
        rank = seen[o]
        seen[o] = rank + 1
        mine = o == me
        rows_of[slot] = j
        slot = slot + jnp.where(mine, 1, 0)
        mail_src[jnp.where(mine, 2 * wide_count, 2 * o + jnp.minimum(rank, 1))] = j

    def from_home(home, slot):
        found = jnp.int32(0)
        for j in range(block_count):
            found = found + jnp.where(owners[j // blocks_z, home, j % blocks_z] == me, 1, 0)
        found = jnp.where(home == me, 0, found)
        for k in range(2):
            rows_of[slot] = block_count + 2 * home + k
            slot = slot + jnp.where(found > k, 1, 0)
        return slot

    slot = lax.fori_loop(0, wide_count, from_home, slot)

    def empty(s, carry):
        rows_of[s] = jnp.where(s < slot, rows_of[s], block_count + 2 * wide_count)
        return carry

    lax.fori_loop(0, capacity, empty, 0)


def body(wide_count, narrow_count, labels, density, velocity, owner_map):
    X, Y, Z = labels.shape
    XE, YE = X + 2 * HALO, Y + 2 * YHALO
    XG, YG = X + 2 * GHALO, Y + 2 * YGHALO
    blocks = (X // BS) * (Z // BS)
    chunks = BS * BS * BS // 128
    per = 4 * chunks
    f32 = jnp.float32
    hbm = pl.BlockSpec(memory_space=pl.ANY)
    smem = pl.BlockSpec(memory_space=pltpu.SMEM)
    capacity = blocks + 2 * (wide_count - 1) - 2 * ((wide_count - 1) // 2)
    mail_src, rows_of = pl.pallas_call(
        functools.partial(routing_kernel, capacity),
        out_shape=[
            jax.ShapeDtypeStruct((2 * wide_count + 1,), jnp.int32),
            jax.ShapeDtypeStruct((capacity + 1,), jnp.int32),
        ],
        in_specs=[smem],
        out_specs=[smem, smem],
        scratch_shapes=[pltpu.SMEM((wide_count,), jnp.int32)],
        name="routing",
    )(owner_map)
    src = pl.pallas_call(
        functools.partial(flow_kernel, wide_count, narrow_count, X, Y),
        out_shape=jax.ShapeDtypeStruct(((blocks + 2 * wide_count) * per, Z), f32),
        in_specs=[hbm, hbm, hbm, pl.BlockSpec(memory_space=pltpu.SMEM)],
        out_specs=hbm,
        scratch_shapes=[
            pltpu.VMEM((4, XE * Y, Z), f32),
            pltpu.VMEM((XG * Y, Z), jnp.int32),
            pltpu.VMEM((XG * Y, Z), f32),
            pltpu.VMEM((XE * Y, Z), f32),
            pltpu.VMEM((4, YE, XE, Z), f32),
            pltpu.VMEM((YG, XE, Z), f32),
            pltpu.VMEM((YE, XE, Z), f32),
            pltpu.VMEM((19, YE, XE, Z), f32),
            pltpu.VMEM((19, YE, XE, Z), f32),
            pltpu.VMEM((4, XE * Y, Z), f32),
            pltpu.VMEM((blocks * per, Z), f32),
            pltpu.VMEM((2 * wide_count * per, Z), f32),
            pltpu.SemaphoreType.DMA((3,)),
            pltpu.SemaphoreType.DMA((6,)),
            pltpu.SemaphoreType.DMA((6,)),
            pltpu.SemaphoreType.DMA((4,)),
            pltpu.SemaphoreType.DMA((4,)),
            pltpu.SemaphoreType.DMA((2 * (STEPS - 1),)),
            pltpu.SemaphoreType.DMA((2 * (STEPS - 1),)),
            pltpu.SemaphoreType.DMA((4 * (wide_count - 1),)),
            pltpu.SemaphoreType.DMA((4 * (wide_count - 1),)),
            pltpu.SemaphoreType.DMA,
        ],
        compiler_params=pltpu.CompilerParams(
            collective_id=0, has_side_effects=True, vmem_limit_bytes=60 * 1024 * 1024
        ),
        name="flow",
    )(labels.reshape(X * Y, Z), density.reshape(1, X * Y, Z), velocity.reshape(3, X * Y, Z), mail_src)
    groups = capacity // 8
    out = pl.pallas_call(
        collect_kernel,
        out_shape=jax.ShapeDtypeStruct((4, groups, chunks * 8, Z), f32),
        grid=(4,),
        in_specs=[
            pl.BlockSpec(memory_space=pltpu.SMEM),
            pl.BlockSpec((blocks + 2 * wide_count, 2, 1, chunks // 2, Z), lambda q: (0, 0, q, 0, 0)),
        ],
        out_specs=pl.BlockSpec((1, groups, chunks * 8, Z), lambda q: (q, 0, 0, 0)),
        compiler_params=pltpu.CompilerParams(vmem_limit_bytes=60 * 1024 * 1024),
        name="collect",
    )(rows_of, src.reshape(blocks + 2 * wide_count, 2, 4, chunks // 2, Z))
    out = out.reshape(4, groups, chunks, 8, Z).transpose(0, 1, 3, 2, 4)
    return out.reshape(4, 1, 1, capacity, BS * BS * BS)


def solution(mesh):
    placed = (
        P("narrow", "wide", None),
        P("narrow", "wide", None),
        P(None, "narrow", "wide", None),
        P("narrow", None, None),
    )
    return jax.shard_map(
        functools.partial(body, mesh.shape["wide"], mesh.shape["narrow"]),
        mesh=mesh,
        in_specs=placed,
        out_specs=P(None, "narrow", "wide", None, None),
        check_vma=False,
    )
```
